256 devices in a mesh: dp: 16 (over x, z_lo), expert: 16 (over z_hi, y, core).
Axes of the slice: x: 4, y: 4, z: 8 (z_hi: 2, z_lo: 4; z = z_hi * 4 + z_lo), core: 2. Of those that a mesh axis runs over, the one named last changes fastest.
Arguments:
- tokens: bfloat16 [8192, 4096], P('expert', 'dp'), may hold values from -6 to 6
- expert_ids: int32 [8192, 2], P('expert'), may hold values from 0 to 31, all different within a row; in each aligned block of 512 rows (0 to 511, 512 to 1023, ...) at most 64 rows name the same one
- gate_values: float32 [8192, 2], P('expert'), may hold values from 0.2 to 1
- w_in: bfloat16 [32, 4096, 1536], P('expert', 'dp'), may hold values from -0.09375 to 0.09375
- w_out: bfloat16 [32, 1536, 4096], P('expert', None, 'dp'), may hold values from -0.15625 to 0.15625
- grad_out: bfloat16 [8192, 4096], P('expert', 'dp'), may hold values from -3 to 3
Outputs:
- mixed: bfloat16 [8192, 4096], P('expert', 'dp')
- grad_tokens: bfloat16 [8192, 4096], P('expert', 'dp')
- grad_w_in: float32 [32, 4096, 1536], P('expert', 'dp')
- grad_w_out: float32 [32, 1536, 4096], P('expert', None, 'dp')
The draws below stay inside these ranges and needn't reach their ends.
Inputs may be any that keep to these rules, and one draw needn't show every extreme that they name: `expert_ids`: each row names 2 different experts; among the 512 rows of one index of expert no expert is named by more than 64 rows, a bound that some block reaches.
All inputs are finite; a program needn't handle non-finite values.
Results may differ from the reference program's by a relative error of at most 0.03.
Values may be sent and summed in bfloat16 or wider, within the bound.
A program may use at most 128 MiB of HBM per device.

```python
import math
import jax
import jax.numpy as jnp
import numpy as np
from jax import lax

D = 4096
H = 1536
TOP = 2
TOK_DEV = 512
EXPERTS = 32
TOKENS = 8192
CAP = 64
N_DP = 16
N_EXPERT = 16


def shard_levels(stream_key, dims, cuts, smallest, high):
    level, own = 1.0, jax.random.fold_in(stream_key, 6)
    for dim, blocks in cuts:
        heights = jnp.exp(jax.random.uniform(jax.random.fold_in(own, dim), (blocks,), jnp.float32, smallest / len(cuts), high / len(cuts)))
        level = level * jnp.repeat(heights, dims[dim] // blocks).reshape([-1 if axis == dim else 1 for axis in range(len(dims))])
    return level


def shared_out(key, own, number, rows, number_of, top, bound, skew):
    order = jax.random.permutation(key, number_of)
    heavy_load, common = portions_of(number_of, rows * top, bound, skew, True), portions_of(number_of, rows * top, bound, skew, False)
    places = jnp.arange(number_of)

    def named(lengths, rotation):
        used = int((lengths > 0).sum())
        fixed = max(1, used // 4)
        shifted = fixed + (places - fixed + rotation * (used - fixed)) % max(1, number_of - fixed)
        return jnp.zeros((number_of,), jnp.int32).at[order[jnp.where(places < fixed, places, shifted)]].set(jnp.asarray(lengths, jnp.int32))

    lengths = jnp.where(number % 4 == 0, named(heavy_load, number // 4), named(common, number - number // 4 - 1))
    mixed = jax.random.permutation(jax.random.fold_in(own, 3), number_of)
    giver, receiver = mixed[0:number_of // 2 * 2:2], mixed[1:number_of // 2 * 2:2]
    room = jnp.minimum(lengths[giver] - 1, bound - lengths[receiver]) // 2
    room = jnp.where((giver == order[0]) | (receiver == order[0]) | (lengths[receiver] == 0), 0, jnp.maximum(room, 0))
    shifted = jax.random.randint(jax.random.fold_in(own, 4), (number_of // 2,), 0, 1 << 20) % (room + 1)
    lengths = lengths.at[giver].add(-shifted).at[receiver].add(shifted)
    items = jnp.searchsorted(jnp.cumsum(lengths), jnp.arange(rows * top), side="right").astype(jnp.int32)
    table = items.reshape(top, rows).T
    table = table[jax.random.permutation(jax.random.fold_in(own, 1), rows)]
    rotation = jax.random.randint(jax.random.fold_in(own, 2), (rows, 1), 0, top)
    return jnp.take_along_axis(table, (jnp.arange(top)[None, :] + rotation) % top, axis=1)


def portions_of(count, total, reach, skew, full):
    weights = [(1 << 20) // math.isqrt(rank ** skew) + 1 for rank in range(1, count + 1)]
    largest = reach if full else min(reach, max(-(-total // count), total * weights[0] // sum(weights)))
    least = 1 if total - largest >= count - 1 else 0
    counts, spare = [largest] + [least] * (count - 1), total - largest - least * (count - 1)
    while spare > 0:
        free = [i for i in range(1, count) if counts[i] < largest] or [i for i in range(1, count) if counts[i] < reach]
        mass, left = sum([weights[i] for i in free]), spare
        for i in free:
            extra = min(reach - counts[i], max(1, left * weights[i] // mass), spare)
            counts[i] = counts[i] + extra
            spare = spare - extra
    return np.array(counts)


def normal_values(stream_key, extent, deviation, reach, shards=(), kind=jnp.bfloat16):
    level = shard_levels(stream_key, extent, shards, -0.22, 0.18) if shards else 1.0
    drawn = jax.random.normal(stream_key, extent, jnp.float32) * deviation * level
    return jnp.minimum(jnp.maximum(drawn, -reach), reach).astype(kind)


def setup_inputs(seed: int = 0) -> dict:
    arg_keys = jax.random.split(jax.random.key(seed), 7)
    tokens = normal_values(arg_keys[0], (TOKENS, D), 1.0, 6.0, ((0, 16), (1, 16)))
    expert_ids_keys = jax.random.split(jax.random.fold_in(arg_keys[1], 1), TOKENS // TOK_DEV)
    expert_ids_turns = jax.random.permutation(jax.random.fold_in(arg_keys[1], 3), TOKENS // TOK_DEV)
    expert_ids = jax.vmap(lambda own, number: shared_out(jax.random.fold_in(arg_keys[1], 2), own, number, TOK_DEV, EXPERTS, TOP, CAP, 2))(expert_ids_keys, expert_ids_turns).reshape((TOKENS, TOP))
    gate_values = jnp.clip(0.2 + 0.8 * jax.random.uniform(arg_keys[2], (TOKENS, TOP), jnp.float32) ** shard_levels(arg_keys[2], (TOKENS, TOP), ((0, 16),), -0.2, 0.2), 0.2, 1.0)
    w_in = normal_values(arg_keys[3], (EXPERTS, D, H), D ** -0.5, 0.09375, ((0, 16), (1, 16)))
    w_out = normal_values(arg_keys[4], (EXPERTS, H, D), H ** -0.5, 0.15625, ((0, 16), (2, 16)))
    grad_out = normal_values(arg_keys[5], (TOKENS, D), 0.5, 3.0, ((0, 16), (1, 16)))
    return dict(tokens=tokens, expert_ids=expert_ids, gate_values=gate_values, w_in=w_in, w_out=w_out, grad_out=grad_out)


def gelu_value(pre):
    return jax.nn.gelu(pre, approximate=True)

def gelu_slope(pre):
    value, pullback = jax.vjp(gelu_value, pre)
    return pullback(jnp.ones_like(pre))[0]

def sliced_product(left, right):
    count = left.shape[0]
    parts = jnp.einsum('rnd,ndh->nrh', left.reshape(count, N_DP, -1).astype(jnp.float32), right.reshape(N_DP, -1, right.shape[1]).astype(jnp.float32))
    rounded = lax.optimization_barrier(parts.astype(jnp.bfloat16))
    return lax.optimization_barrier(jnp.sum(rounded.astype(jnp.float32), axis=0))

def reference(tokens, expert_ids, gate_values, w_in, w_out, grad_out):
    groups = N_EXPERT
    ids = expert_ids.reshape(groups, TOK_DEV * TOP)
    onehot = (ids[:, :, None] == jnp.arange(EXPERTS, dtype=jnp.int32)[None, None, :]).astype(jnp.int32)
    position = lax.optimization_barrier(jnp.sum((jnp.cumsum(onehot, axis=1) - onehot) * onehot, axis=2))
    source = jnp.arange(groups, dtype=jnp.int32)[:, None]
    target = ((ids * groups + source) * CAP + position).reshape(-1).astype(jnp.int32)
    pair_rows = jnp.repeat(tokens, TOP, axis=0)
    scaled = (gate_values[:, :, None] * grad_out[:, None, :].astype(jnp.float32)).astype(jnp.bfloat16).reshape(TOKENS * TOP, D)
    bucket_rows = jnp.zeros((EXPERTS * groups * CAP, D), jnp.bfloat16).at[target].set(pair_rows).reshape(EXPERTS, groups * CAP, D)
    bucket_grads = jnp.zeros((EXPERTS * groups * CAP, D), jnp.bfloat16).at[target].set(scaled).reshape(EXPERTS, groups * CAP, D)

    def one_expert(operands):
        rows, grads, weight_in, weight_out = operands
        pre = sliced_product(rows, weight_in)
        act = gelu_value(pre).astype(jnp.bfloat16)
        result = jnp.dot(act, weight_out, preferred_element_type=jnp.float32).astype(jnp.bfloat16)
        slope = sliced_product(grads, weight_out.T)
        delta = (slope * gelu_slope(pre)).astype(jnp.bfloat16)
        grad_out_w = jnp.dot(act.T, grads, preferred_element_type=jnp.float32)
        grad_in_w = jnp.dot(rows.T, delta, preferred_element_type=jnp.float32)
        back = jnp.dot(delta, weight_in.T, preferred_element_type=jnp.float32).astype(jnp.bfloat16)
        return (result, back, grad_in_w, grad_out_w)
    result, back, grad_w_in, grad_w_out = lax.map(one_expert, (bucket_rows, bucket_grads, w_in, w_out))
    picked = result.reshape(-1, D)[target].reshape(TOKENS, TOP, D).astype(jnp.float32)
    mixed = lax.optimization_barrier(jnp.sum(gate_values[:, :, None] * picked, axis=1)).astype(jnp.bfloat16)
    returned = back.reshape(-1, D)[target].reshape(TOKENS, TOP, D).astype(jnp.float32)
    grad_tokens = lax.optimization_barrier(jnp.sum(returned, axis=1)).astype(jnp.bfloat16)
    return (mixed, grad_tokens, grad_w_in, grad_w_out)
```

```python
import jax
import jax.numpy as jnp
from jax import lax
from jax.sharding import PartitionSpec as P

TOP = 2
EXP_DEV = 2


def gelu_value(pre):
    return jax.nn.gelu(pre, approximate=True)


def gelu_slope(pre):
    value, pullback = jax.vjp(gelu_value, pre)
    return pullback(jnp.ones_like(pre))[0]


def slot_index(expert_ids, num_experts, capacity):
    flat = expert_ids.reshape(-1)
    onehot = flat[:, None] == jnp.arange(num_experts, dtype=jnp.int32)[None, :]
    order = jnp.arange(flat.shape[0], dtype=jnp.int32)
    earlier = (order[None, :] < order[:, None]).astype(jnp.bfloat16)
    before = jnp.dot(earlier, onehot.astype(jnp.bfloat16), preferred_element_type=jnp.float32)
    position = jnp.sum(jnp.where(onehot, before, 0.0), axis=1).astype(jnp.int32)
    return flat * capacity + position


def sum_apart(partial_value):
    return lax.psum_scatter(
        partial_value.astype(jnp.bfloat16), "dp", scatter_dimension=0, tiled=True
    ).astype(jnp.float32)


def gather_apart(share):
    return lax.all_gather(share, "dp", axis=0, tiled=True)


def send_back(slot_rows):
    return lax.all_to_all(slot_rows, "expert", split_axis=0, concat_axis=0, tiled=True)


def body(tokens, expert_ids, gate_values, w_in, w_out, grad_out):
    groups = lax.axis_size("expert")
    tok_rows = tokens.shape[0]
    width = tokens.shape[1]
    hidden = w_in.shape[2]
    num_experts = EXP_DEV * groups
    capacity = 2 * tok_rows * TOP // num_experts
    total = num_experts * capacity
    slots = slot_index(expert_ids, num_experts, capacity)
    pair_rows = jnp.repeat(tokens, TOP, axis=0)
    scaled = (
        (gate_values[:, :, None] * grad_out[:, None, :].astype(jnp.float32))
        .astype(jnp.bfloat16)
        .reshape(tok_rows * TOP, width)
    )
    send_rows = (
        jnp.zeros((total, width), jnp.bfloat16)
        .at[slots]
        .set(pair_rows)
        .reshape(groups, EXP_DEV * capacity, width)
    )
    send_grads = (
        jnp.zeros((total, width), jnp.bfloat16)
        .at[slots]
        .set(scaled)
        .reshape(groups, EXP_DEV * capacity, width)
    )

    def inbound(rows):
        return rows.reshape(groups, EXP_DEV, capacity, width)

    got_rows = inbound(lax.all_to_all(send_rows, "expert", split_axis=0, concat_axis=0, tiled=True))
    pre_share = sum_apart(
        jnp.einsum("slcd,ldh->slch", got_rows, w_in, preferred_element_type=jnp.float32).reshape(
            -1, hidden
        )
    )
    act = gather_apart(gelu_value(pre_share).astype(jnp.bfloat16)).reshape(
        groups, EXP_DEV, capacity, hidden
    )
    result = jnp.einsum("slch,lhd->slcd", act, w_out, preferred_element_type=jnp.float32).astype(
        jnp.bfloat16
    )
    arrived = send_back(result.reshape(groups, EXP_DEV * capacity, width)).reshape(total, width)
    picked = arrived[slots].reshape(tok_rows, TOP, width).astype(jnp.float32)
    mixed = jnp.sum(gate_values[:, :, None] * picked, axis=1).astype(jnp.bfloat16)
    got_grads = inbound(
        lax.all_to_all(send_grads, "expert", split_axis=0, concat_axis=0, tiled=True)
    )
    slope_share = sum_apart(
        jnp.einsum("slcd,lhd->slch", got_grads, w_out, preferred_element_type=jnp.float32).reshape(
            -1, hidden
        )
    )
    delta = gather_apart((slope_share * gelu_slope(pre_share)).astype(jnp.bfloat16)).reshape(
        groups, EXP_DEV, capacity, hidden
    )
    grad_w_out = jnp.einsum("slch,slcd->lhd", act, got_grads, preferred_element_type=jnp.float32)
    grad_w_in = jnp.einsum("slcd,slch->ldh", got_rows, delta, preferred_element_type=jnp.float32)
    back = jnp.einsum("slch,ldh->slcd", delta, w_in, preferred_element_type=jnp.float32).astype(
        jnp.bfloat16
    )
    returned = send_back(back.reshape(groups, EXP_DEV * capacity, width)).reshape(total, width)
    gathered = returned[slots].reshape(tok_rows, TOP, width).astype(jnp.float32)
    grad_tokens = jnp.sum(gathered, axis=1).astype(jnp.bfloat16)
    return (mixed, grad_tokens, grad_w_in, grad_w_out)


def solution(mesh):
    return jax.shard_map(
        body,
        mesh=mesh,
        in_specs=(
            P("expert", "dp"),
            P("expert", None),
            P("expert", None),
            P("expert", "dp", None),
            P("expert", None, "dp"),
            P("expert", "dp"),
        ),
        out_specs=(
            P("expert", "dp"),
            P("expert", "dp"),
            P("expert", "dp", None),
            P("expert", None, "dp"),
        ),
        check_vma=False,
    )
```

```python
import functools

import jax
import jax.numpy as jnp
from jax import lax
from jax.experimental import pallas as pl
from jax.experimental.pallas import tpu as pltpu
from jax.sharding import PartitionSpec as P

TOP = 2
EXP_DEV = 2
MESH = pl.DeviceIdType.MESH
GROUPS = (
    (0, 640, (0, 1, 2, 3)),
    (640, 640, (1, 0, 2, 3)),
    (1280, 128, (2, 3, 0, 1)),
    (1408, 128, (2, 3, 1, 0)),
)
STEPS = 4
TILE = 128


def gelu_value(pre):
    return jax.nn.gelu(pre, approximate=True)


def gelu_parts(pre):
    scale, cubic = 0.7978845608028654, 0.044715
    square = pre * pre
    tanh = jnp.tanh(scale * (pre + cubic * square * pre))
    half = 0.5 * (1.0 + tanh)
    slope = half + 0.5 * pre * (1.0 - tanh * tanh) * (scale * (1.0 + 3.0 * cubic * square))
    return pre * half, slope


def slot_index(expert_ids, num_experts, capacity):
    flat = expert_ids.reshape(-1)
    onehot = flat[:, None] == jnp.arange(num_experts, dtype=jnp.int32)[None, :]
    order = jnp.arange(flat.shape[0], dtype=jnp.int32)
    earlier = (order[None, :] < order[:, None]).astype(jnp.bfloat16)
    before = jnp.dot(earlier, onehot.astype(jnp.bfloat16), preferred_element_type=jnp.float32)
    position = jnp.sum(jnp.where(onehot, before, 0.0), axis=1).astype(jnp.int32)
    return flat * capacity + position


def partners_of(dp):
    x, z = dp // 4, dp % 4
    x0, x1, z0, z1 = x % 2, x // 2, z % 2, z // 2
    flip = lambda b: 1 - b
    at = lambda a1, a0, c1, c0: (a1 * 2 + a0) * 4 + c1 * 2 + c0
    return (
        (at(x1, flip(x0), z1, z0), (x0 + x1) % 2),
        (at(flip(x1), flip(x0), z1, z0), x1),
        (at(x1, x0, z1, flip(z0)), z0),
        (at(x1, x0, flip(z1), z0), z1),
    )


def hidden_kernel(rows_ref, grads_ref, w_in_ref, w_out_ref, act_ref, delta_ref, *scratch):
    count = len(GROUPS)
    work = (scratch[0:count], scratch[count : 2 * count])
    recv = (scratch[2 * count : 3 * count], scratch[3 * count : 4 * count])
    rs_send, rs_recv, ag_send, ag_recv = scratch[4 * count :]
    dp, ex = lax.axis_index("dp"), lax.axis_index("expert")
    partners = partners_of(dp)
    total = rows_ref.shape[0]
    per_expert = total // EXP_DEV
    outs = (act_ref, delta_ref)

    barrier = pltpu.get_barrier_semaphore()
    for other, _ in partners:
        pl.semaphore_signal(barrier, inc=1, device_id=(other, ex), device_id_type=MESH)

    def partial_products(tensor, g):
        first, columns, _ = GROUPS[g]
        tile = 256

        def body(i, carry):
            at = pl.ds(pl.multiple_of(i * tile, tile), tile)
            expert = i // (per_expert // tile)
            if tensor == 0:
                value = jnp.dot(
                    rows_ref[at, :],
                    w_in_ref[expert, :, first : first + columns],
                    preferred_element_type=jnp.float32,
                )
            else:
                value = lax.dot_general(
                    grads_ref[at, :],
                    w_out_ref[expert, first : first + columns, :],
                    (((1,), (1,)), ((), ())),
                    preferred_element_type=jnp.float32,
                )
            work[tensor][g][at, :] = value.astype(jnp.bfloat16)
            return carry

        lax.fori_loop(0, total // tile, body, 0)

    offsets = [[0] for _ in GROUPS]
    for g, (_, _, order) in enumerate(GROUPS):
        for k in range(STEPS):
            offsets[g].append(offsets[g][k] + partners[order[k]][1] * (total >> (k + 1)))

    def rs_copy(tensor, g, k):
        other, bit = partners[GROUPS[g][2][k]]
        size = total >> (k + 1)
        start = pl.multiple_of(offsets[g][k] + (1 - bit) * size, TILE)
        return pltpu.make_async_remote_copy(
            src_ref=work[tensor][g].at[pl.ds(start, size), :],
            dst_ref=recv[tensor][g].at[pl.ds(total - 2 * size, size), :],
            send_sem=rs_send.at[tensor, g, k],
            recv_sem=rs_recv.at[tensor, g, k],
            device_id=(other, ex),
            device_id_type=MESH,
        )

    def ag_copy(tensor, g, k):
        other, _ = partners[GROUPS[g][2][k]]
        first, columns, _ = GROUPS[g]
        size = total >> (k + 1)
        held = outs[tensor].at[
            pl.ds(pl.multiple_of(offsets[g][k + 1], TILE), size), pl.ds(first, columns)
        ]
        return pltpu.make_async_remote_copy(
            src_ref=held,
            dst_ref=held,
            send_sem=ag_send.at[tensor, g, k],
            recv_sem=ag_recv.at[tensor, g, k],
            device_id=(other, ex),
            device_id_type=MESH,
        )

    def add(tensor, g, k):
        size = total >> (k + 1)
        tile = 64

        def body(i, carry):
            at = pl.ds(pl.multiple_of(offsets[g][k + 1] + i * tile, tile), tile)
            came = pl.ds(pl.multiple_of(total - 2 * size + i * tile, tile), tile)
            mine = work[tensor][g][at, :].astype(jnp.float32)
            work[tensor][g][at, :] = (
                mine + recv[tensor][g][came, :].astype(jnp.float32)
            ).astype(jnp.bfloat16)
            return carry

        lax.fori_loop(0, size // tile, body, 0)

    def activate(g):
        first, columns, _ = GROUPS[g]
        k = STEPS - 1
        size = total >> STEPS
        tile = 32

        def body(i, carry):
            at = pl.ds(pl.multiple_of(offsets[g][STEPS] + i * tile, tile), tile)
            came = pl.ds(pl.multiple_of(total - 2 * size + i * tile, tile), tile)
            for c in range(0, columns, 128):
                here = slice(c, c + 128)
                pre = work[0][g][at, here].astype(jnp.float32) + recv[0][g][came, here].astype(jnp.float32)
                rise = work[1][g][at, here].astype(jnp.float32) + recv[1][g][came, here].astype(jnp.float32)
                value, slope = gelu_parts(pre)
                act_ref[at, first + c : first + c + 128] = value.astype(jnp.bfloat16)
                delta_ref[at, first + c : first + c + 128] = (rise * slope).astype(jnp.bfloat16)
            return carry

        lax.fori_loop(0, size // tile, body, 0)

    todo = [(tensor, g) for tensor in (0, 1) for g in (2, 3, 0, 1)]
    for n, (tensor, g) in enumerate(todo):
        partial_products(tensor, g)
        if n == 0:
            pl.semaphore_wait(barrier, len(partners))
        rs_copy(tensor, g, 0).start()
    for k in range(STEPS):
        for tensor, g in todo:
            rs_copy(tensor, g, k).wait_recv()
            if k < STEPS - 1:
                add(tensor, g, k)
                rs_copy(tensor, g, k + 1).start()
    for _, g in todo[: len(GROUPS)]:
        activate(g)
        for tensor in (0, 1):
            ag_copy(tensor, g, STEPS - 1).start()
    for k in reversed(range(STEPS)):
        for tensor, g in todo:
            ag_copy(tensor, g, k).wait_recv()
            if k:
                ag_copy(tensor, g, k - 1).start()
    for k in range(STEPS):
        for tensor, g in todo:
            rs_copy(tensor, g, k).wait_send()
            ag_copy(tensor, g, k).wait_send()


def hidden(rows, grads, w_in, w_out):
    total, units = rows.shape[0], w_in.shape[2]
    out = jax.ShapeDtypeStruct((total, units), jnp.bfloat16)
    pair = [pltpu.VMEM((total, c), jnp.bfloat16) for _, c, _ in GROUPS]
    came = [pltpu.VMEM((total - total // 16, c), jnp.bfloat16) for _, c, _ in GROUPS]
    return pl.pallas_call(
        hidden_kernel,
        out_shape=(out, out),
        in_specs=[pl.BlockSpec(memory_space=pltpu.VMEM)] * 4,
        out_specs=[pl.BlockSpec(memory_space=pltpu.VMEM)] * 2,
        scratch_shapes=pair * 2 + came * 2 + [pltpu.SemaphoreType.DMA((2, len(GROUPS), STEPS))] * 4,
        compiler_params=pltpu.CompilerParams(
            collective_id=0, has_side_effects=True, vmem_limit_bytes=52 * 2**20
        ),
        name="hidden",
    )(rows, grads, w_in, w_out)


def exchange(slot_rows):
    return lax.all_to_all(slot_rows, "expert", split_axis=0, concat_axis=0, tiled=True)


def body(tokens, expert_ids, gate_values, w_in, w_out, grad_out):
    groups = lax.axis_size("expert")
    tok_rows, width = tokens.shape
    num_experts = EXP_DEV * groups
    capacity = 2 * tok_rows * TOP // num_experts
    total = num_experts * capacity
    slots = slot_index(expert_ids, num_experts, capacity)
    pair_rows = jnp.repeat(tokens, TOP, axis=0)
    scaled = (
        (gate_values[:, :, None] * grad_out[:, None, :].astype(jnp.float32))
        .astype(jnp.bfloat16)
        .reshape(tok_rows * TOP, width)
    )

    def dispatch(rows):
        sent = jnp.zeros((total, width), jnp.bfloat16).at[slots].set(rows)
        got = exchange(sent.reshape(groups, EXP_DEV * capacity, width))
        return got.reshape(groups, EXP_DEV, capacity, width).transpose(1, 0, 2, 3).reshape(total, width)

    def send_back(rows):
        by_source = rows.reshape(EXP_DEV, groups, capacity, width).transpose(1, 0, 2, 3)
        back = exchange(by_source.reshape(groups, EXP_DEV * capacity, width)).reshape(total, width)
        return back[slots].reshape(tok_rows, TOP, width).astype(jnp.float32)

    rows, grads = dispatch(pair_rows), dispatch(scaled)
    act, delta = hidden(rows, grads, w_in, w_out)
    by_expert = lambda a: a.reshape(EXP_DEV, groups * capacity, -1)
    act, delta, rows, grads = by_expert(act), by_expert(delta), by_expert(rows), by_expert(grads)
    product = functools.partial(jnp.einsum, preferred_element_type=jnp.float32)
    result = product("lrh,lhd->lrd", act, w_out).astype(jnp.bfloat16)
    back = product("lrh,ldh->lrd", delta, w_in).astype(jnp.bfloat16)
    mixed = jnp.sum(gate_values[:, :, None] * send_back(result), axis=1).astype(jnp.bfloat16)
    grad_tokens = jnp.sum(send_back(back), axis=1).astype(jnp.bfloat16)
    grad_w_out = product("lrh,lrd->lhd", act, grads)
    grad_w_in = product("lrd,lrh->ldh", rows, delta)
    return (mixed, grad_tokens, grad_w_in, grad_w_out)


def solution(mesh):
    return jax.shard_map(
        body,
        mesh=mesh,
        in_specs=(
            P("expert", "dp"),
            P("expert", None),
            P("expert", None),
            P("expert", "dp", None),
            P("expert", None, "dp"),
            P("expert", "dp"),
        ),
        out_specs=(
            P("expert", "dp"),
            P("expert", "dp"),
            P("expert", "dp", None),
            P("expert", None, "dp"),
        ),
        check_vma=False,
    )
```

```python
import functools

import jax
import jax.numpy as jnp
from jax import lax
from jax.experimental import pallas as pl
from jax.experimental.pallas import tpu as pltpu
from jax.sharding import PartitionSpec as P

TOP = 2
EXP_DEV = 2
MESH = pl.DeviceIdType.MESH
STEPS = 4
MATES = 8
GROUPS = (
    (256, (2, 0, 1, 3)),
    (256, (2, 1, 0, 3)),
    (256, (1, 0, 2, 3)),
    (256, (0, 1, 2, 3)),
    (256, (0, 1, 2, 3)),
    (256, (1, 0, 2, 3)),
)
FIRST = tuple(sum(c for c, _ in GROUPS[:g]) for g in range(len(GROUPS)))
ORDER = (
    80, 88, 48, 56, 64, 72, 176, 32, 184, 40, 168, 89, 144, 8, 160, 81, 152, 0, 185, 49, 177, 57, 128, 65,
    136, 33, 104, 90, 145, 41, 96, 82, 153, 9, 161, 1, 129, 50, 186, 34, 91, 178, 83, 66, 187, 137, 58, 146,
    51, 73, 105, 16, 179, 97, 10, 130, 35, 42, 162, 154, 24, 147, 59, 131, 39, 106, 138, 155, 43, 169, 2, 74,
    135, 38, 11, 139, 47, 120, 107, 63, 98, 25, 112, 17, 143, 3, 170, 46, 134, 37, 159, 62, 67, 99, 55, 121,
    26, 113, 163, 75, 142, 45, 18, 158, 61, 133, 36, 151, 54, 87, 171, 95, 183, 7, 122, 86, 150, 157, 114, 60,
    141, 44, 53, 191, 15, 103, 6, 19, 182, 94, 111, 27, 115, 23, 102, 85, 132, 5, 149, 14, 123, 31, 119, 71,
    190, 22, 110, 93, 127, 79, 167, 140, 13, 181, 101, 84, 175, 118, 30, 109, 156, 70, 189, 21, 92, 126, 29,
    78, 166, 52, 174, 4, 117, 69, 180, 125, 28, 20, 188, 77, 165, 148, 12, 100, 124, 173, 76, 68, 116, 108,
    172, 164,
)


def decoded(number):
    rest, k = divmod(number, STEPS)
    rest, gather = divmod(rest, 2)
    rest, g = divmod(rest, len(GROUPS))
    wait, tensor = divmod(rest, 2)
    return wait, tensor, g, gather, k


def gelu_parts(pre):
    scale, cubic = 0.7978845608028654, 0.044715
    square = pre * pre
    tanh = jnp.tanh(scale * (pre + cubic * square * pre))
    half = 0.5 * (1.0 + tanh)
    slope = half + 0.5 * pre * (1.0 - tanh * tanh) * (scale * (1.0 + 3.0 * cubic * square))
    return pre * half, slope


def slot_index(expert_ids, num_experts, capacity):
    flat = expert_ids.reshape(-1)
    onehot = flat[:, None] == jnp.arange(num_experts, dtype=jnp.int32)[None, :]
    order = jnp.arange(flat.shape[0], dtype=jnp.int32)
    earlier = (order[None, :] < order[:, None]).astype(jnp.bfloat16)
    before = jnp.dot(earlier, onehot.astype(jnp.bfloat16), preferred_element_type=jnp.float32)
    position = jnp.sum(jnp.where(onehot, before, 0.0), axis=1).astype(jnp.int32)
    return flat * capacity + position


def partners_of(dp):
    x, z = dp // 4, dp % 4
    x0, x1, z0, z1 = x % 2, x // 2, z % 2, z // 2

    def at(a1, a0, c1, c0):
        return (a1 * 2 + a0) * 4 + c1 * 2 + c0

    return (
        (at(x1, 1 - x0, z1, z0), (x0 + x1) % 2),
        (at(1 - x1, 1 - x0, z1, z0), x1),
        (at(x1, x0, z1, 1 - z0), z0),
        (at(x1, x0, 1 - z1, z0), z1),
    )


def layer_kernel(
    tokens_ref, grad_out_ref, info_ref, w_in_ref, w_out_ref, mixed_ref, grad_tokens_ref, gw_in_ref, gw_out_ref, *scratch
):
    count = len(GROUPS)
    work = (scratch[0:count], scratch[count : 2 * count])
    recv = (scratch[2 * count : 3 * count], scratch[3 * count : 4 * count])
    (
        act_ref, delta_ref, rows_ref, grads_ref, info_other, tokens_other, grad_out_other, hot, gate,
        sent, ret, half_sent, half_came,
        rs_send, rs_recv, ag_send, ag_recv, y_send, y_recv, b_send, b_recv, h_send, h_recv,
    ) = scratch[4 * count :]
    dp, ex = lax.axis_index("dp"), lax.axis_index("expert")
    zh, mate = ex // MATES, ex % MATES
    across = (1 - zh) * MATES + mate
    partners = partners_of(dp)
    tok_rows, width = tokens_ref.shape
    per_expert = rows_ref.shape[1]
    total = EXP_DEV * per_expert
    units = act_ref.shape[1]
    cap = per_expert // (2 * MATES)
    outs = (act_ref, delta_ref)
    routed = (rows_ref, grads_ref)

    barrier = pltpu.get_barrier_semaphore()
    for other, _ in partners:
        pl.semaphore_signal(barrier, inc=1, device_id=(other, ex), device_id_type=MESH)
    pl.semaphore_signal(barrier, inc=1, device_id=(dp, across), device_id_type=MESH)
    for j in range(1, MATES):
        near = zh * MATES + (mate + j) % MATES
        pl.semaphore_signal(barrier, inc=1, device_id=(dp, near), device_id_type=MESH)

    def build_map(b):
        source = info_ref if b == 0 else info_other
        tile = 128

        def body(i, carry):
            at = pl.ds(pl.multiple_of(i * tile, tile), tile)
            slot = (
                lax.broadcasted_iota(jnp.int32, (tile, tok_rows), 0) + (zh * per_expert + i * tile)
            ).astype(jnp.float32)
            first, second = source[0:1, :] == slot, source[1:2, :] == slot
            hot[b, at, :] = jnp.where(first, 1.0, jnp.where(second, 1.0, 0.0)).astype(jnp.bfloat16)
            weight = jnp.where(first, source[2:3, :], jnp.where(second, source[3:4, :], 0.0))
            gate[b, at, :] = jnp.broadcast_to(jnp.sum(weight, axis=1, keepdims=True), (tile, 128))
            return carry

        lax.fori_loop(0, per_expert // tile, body, 0)

    def here(b):
        return zh if b == 0 else 1 - zh

    def piece(owner, b):
        return pl.ds(pl.multiple_of((owner * 2 + here(b)) * cap, cap), cap)

    def route_copy(tensor, b, j):
        to = (mate + j) % MATES
        return pltpu.make_async_remote_copy(
            src_ref=sent.at[tensor, :, piece(to, b), :],
            dst_ref=routed[tensor].at[:, piece(mate, b), :],
            send_sem=y_send.at[tensor, b, j],
            recv_sem=y_recv.at[tensor, b, j],
            device_id=(dp, zh * MATES + to),
            device_id_type=MESH,
        )

    def route_wait(tensor, b, j):
        return route_copy(tensor, b, j).wait_recv()

    def dispatch(tensor, b):
        block = ((tokens_ref, grad_out_ref), (tokens_other, grad_out_other))[b][tensor]
        near = 4

        def body(i, carry):
            at = pl.ds(pl.multiple_of(i * near * 2 * cap, near * 2 * cap), near * 2 * cap)
            picked = jnp.dot(hot[b, at, :], block[...], preferred_element_type=jnp.float32)
            if tensor == 1:
                level = gate[b, at, :]
                picked = picked * jnp.concatenate([level] * (width // 128), axis=1)
            picked = picked.astype(jnp.bfloat16)
            for n in range(near):
                for e in range(EXP_DEV):
                    start = (n * EXP_DEV + e) * cap
                    sent[tensor, e, piece(i * near + n, b), :] = picked[start : start + cap, :]
            return carry

        lax.fori_loop(0, MATES // near, body, 0)

        def go(j, carry):
            route_copy(tensor, b, j).start()
            return carry

        lax.fori_loop(1, MATES, go, 0)
        routed[tensor][:, piece(mate, b), :] = sent[tensor, :, piece(mate, b), :]

    def arrived(tensor, b):
        def body(j, carry):
            route_wait(tensor, b, j)
            return carry

        lax.fori_loop(1, MATES, body, 0)

    def across_copy(n, source, target):
        return pltpu.make_async_remote_copy(
            src_ref=source,
            dst_ref=target,
            send_sem=h_send.at[n],
            recv_sem=h_recv.at[n],
            device_id=(dp, across),
            device_id_type=MESH,
        )

    def partial_products(tensor, g):
        columns, _ = GROUPS[g]
        first = FIRST[g]
        tile = 512

        def body(i, carry):
            expert = i // (per_expert // tile)
            inner = pl.ds(pl.multiple_of((i % (per_expert // tile)) * tile, tile), tile)
            if tensor == 0:
                value = jnp.dot(
                    rows_ref[expert, inner, :],
                    w_in_ref[expert, :, first : first + columns],
                    preferred_element_type=jnp.float32,
                )
            else:
                value = lax.dot_general(
                    grads_ref[expert, inner, :],
                    w_out_ref[expert, first : first + columns, :],
                    (((1,), (1,)), ((), ())),
                    preferred_element_type=jnp.float32,
                )
            work[tensor][g][pl.ds(pl.multiple_of(i * tile, tile), tile), :] = value.astype(jnp.bfloat16)
            return carry

        lax.fori_loop(0, total // tile, body, 0)

    offsets = [[0] for _ in GROUPS]
    for g, (_, order) in enumerate(GROUPS):
        for k in range(STEPS):
            offsets[g].append(offsets[g][k] + partners[order[k]][1] * (total >> (k + 1)))

    def rs_copy(tensor, g, k):
        other, bit = partners[GROUPS[g][1][k]]
        size = total >> (k + 1)
        start = pl.multiple_of(offsets[g][k] + (1 - bit) * size, 128)
        return pltpu.make_async_remote_copy(
            src_ref=work[tensor][g].at[pl.ds(start, size), :],
            dst_ref=recv[tensor][g].at[pl.ds(total - 2 * size, size), :],
            send_sem=rs_send.at[tensor, g, k],
            recv_sem=rs_recv.at[tensor, g, k],
            device_id=(other, ex),
            device_id_type=MESH,
        )

    def ag_copy(tensor, g, k):
        other, _ = partners[GROUPS[g][1][k]]
        size = total >> (k + 1)
        held = outs[tensor].at[
            pl.ds(pl.multiple_of(offsets[g][k + 1], 128), size), pl.ds(FIRST[g], GROUPS[g][0])
        ]
        return pltpu.make_async_remote_copy(
            src_ref=held,
            dst_ref=held,
            send_sem=ag_send.at[tensor, g, k],
            recv_sem=ag_recv.at[tensor, g, k],
            device_id=(other, ex),
            device_id_type=MESH,
        )

    def add(tensor, g, k):
        size = total >> (k + 1)
        tile = 128

        def body(i, carry):
            at = pl.ds(pl.multiple_of(offsets[g][k + 1] + i * tile, tile), tile)
            came = pl.ds(pl.multiple_of(total - 2 * size + i * tile, tile), tile)
            mine = work[tensor][g][at, :].astype(jnp.float32)
            work[tensor][g][at, :] = (
                mine + recv[tensor][g][came, :].astype(jnp.float32)
            ).astype(jnp.bfloat16)
            return carry

        lax.fori_loop(0, size // tile, body, 0)

    def activate(g):
        columns, _ = GROUPS[g]
        size = total >> STEPS
        tile = 32

        def body(i, carry):
            at = pl.ds(pl.multiple_of(offsets[g][STEPS] + i * tile, tile), tile)
            came = pl.ds(pl.multiple_of(total - 2 * size + i * tile, tile), tile)
            for c in range(0, columns, 128):
                part = slice(c, c + 128)
                there = slice(FIRST[g] + c, FIRST[g] + c + 128)
                pre = work[0][g][at, part].astype(jnp.float32) + recv[0][g][came, part].astype(jnp.float32)
                rise = work[1][g][at, part].astype(jnp.float32) + recv[1][g][came, part].astype(jnp.float32)
                value, slope = gelu_parts(pre)
                act_ref[at, there] = value.astype(jnp.bfloat16)
                delta_ref[at, there] = (rise * slope).astype(jnp.bfloat16)
            return carry

        lax.fori_loop(0, size // tile, body, 0)

    def back_copy(tensor, b, j):
        to = (mate + j) % MATES
        return pltpu.make_async_remote_copy(
            src_ref=sent.at[tensor, :, piece(to, b), :],
            dst_ref=ret.at[tensor, b, mate],
            send_sem=b_send.at[tensor, b, j],
            recv_sem=b_recv.at[tensor, b, j],
            device_id=(dp, zh * MATES + to),
            device_id_type=MESH,
        )

    def results(tensor):
        tile = 512

        def body(i, carry):
            expert = i // (per_expert // tile)
            inner = pl.ds(pl.multiple_of((i % (per_expert // tile)) * tile, tile), tile)
            at = pl.ds(pl.multiple_of(i * tile, tile), tile)
            if tensor == 0:
                value = jnp.dot(act_ref[at, :], w_out_ref[expert], preferred_element_type=jnp.float32)
            else:
                value = lax.dot_general(
                    delta_ref[at, :],
                    w_in_ref[expert],
                    (((1,), (1,)), ((), ())),
                    preferred_element_type=jnp.float32,
                )
            sent[tensor, expert, inner, :] = value.astype(jnp.bfloat16)
            return carry

        lax.fori_loop(0, total // tile, body, 0)
        for b in (1, 0):

            def go(j, carry):
                back_copy(tensor, b, j).start()
                return carry

            lax.fori_loop(1, MATES, go, 0)
            ret[tensor, b, mate] = sent[tensor, :, piece(mate, b), :]

    def combine(tensor, b):
        def body(j, carry):
            back_copy(tensor, b, j).wait_recv()
            return carry

        lax.fori_loop(1, MATES, body, 0)
        value = ret[tensor, b].reshape(per_expert, width)
        over_slots = (((0,), (0,)), ((), ()))
        if tensor == 1:
            return lax.dot_general(hot[b], value, over_slots, preferred_element_type=jnp.float32)
        level = gate[b]
        value = value.astype(jnp.float32) * jnp.concatenate([level] * (width // 128), axis=1)
        high = value.astype(jnp.bfloat16)
        low = (value - high.astype(jnp.float32)).astype(jnp.bfloat16)
        return lax.dot_general(
            hot[b], high, over_slots, preferred_element_type=jnp.float32
        ) + lax.dot_general(hot[b], low, over_slots, preferred_element_type=jnp.float32)

    def half_copy(tensor):
        return across_copy(3 + tensor, half_sent.at[tensor], half_came.at[tensor])

    def combine_other(tensor):
        half_sent[tensor] = combine(tensor, 1).astype(jnp.bfloat16)
        half_copy(tensor).start()

    def combine_own(tensor, out_ref):
        mine = combine(tensor, 0)
        half_copy(tensor).wait_recv()
        out_ref[...] = (mine + half_came[tensor].astype(jnp.float32)).astype(jnp.bfloat16)

    def weight_gradient_out(expert):
        tile = 256
        rows = pl.ds(expert * per_expert, per_expert)

        def body(i, carry):
            columns = pl.ds(pl.multiple_of(i * tile, tile), tile)
            gw_out_ref[expert, columns, :] = lax.dot_general(
                act_ref[rows, columns],
                grads_ref[expert],
                (((0,), (0,)), ((), ())),
                preferred_element_type=jnp.float32,
            )
            return carry

        lax.fori_loop(0, units // tile, body, 0)

    def weight_gradient_in(expert):
        tile = 256
        rows = pl.ds(expert * per_expert, per_expert)

        def body(i, carry):
            columns = pl.ds(pl.multiple_of(i * tile, tile), tile)
            gw_in_ref[expert, :, columns] = lax.dot_general(
                rows_ref[expert],
                delta_ref[rows, columns],
                (((0,), (0,)), ((), ())),
                preferred_element_type=jnp.float32,
            )
            return carry

        lax.fori_loop(0, units // tile, body, 0)

    pl.semaphore_wait(barrier, len(partners) + MATES)
    info_copy = across_copy(0, info_ref, info_other)
    grad_copy = across_copy(1, grad_out_ref, grad_out_other)
    token_copy = across_copy(2, tokens_ref, tokens_other)
    info_copy.start()
    grad_copy.start()
    token_copy.start()
    build_map(0)
    dispatch(1, 0)
    dispatch(0, 0)
    info_copy.wait_recv()
    build_map(1)
    grad_copy.wait_recv()
    dispatch(1, 1)
    for b in (0, 1):
        arrived(1, b)

    multiplied = set()
    for number in ORDER:
        wait, tensor, g, gather, k = decoded(number)
        if not wait and not gather and k == 0:
            if tensor == 0 and not multiplied & {(0, n) for n in range(count)}:
                token_copy.wait_recv()
                dispatch(0, 1)
                for b in (0, 1):
                    arrived(0, b)
            multiplied.add((tensor, g))
            partial_products(tensor, g)
        copy = (ag_copy if gather else rs_copy)(tensor, g, k)
        if not wait:
            copy.start()
            continue
        copy.wait_recv()
        if gather:
            multiplied.add((tensor, g, k))
            if k == 0 and tensor == 0 and all((0, n, 0) in multiplied for n in range(count)):
                for b in (0, 1):

                    def left(j, carry):
                        for t in (0, 1):
                            route_copy(t, b, j).wait_send()
                        return carry

                    lax.fori_loop(1, MATES, left, 0)
                results(0)
        elif k < STEPS - 1:
            add(tensor, g, k)
        else:
            multiplied.add((tensor, g, "summed"))
            if all((t, g, "summed") in multiplied for t in (0, 1)):
                activate(g)

    results(1)
    for expert in range(EXP_DEV):
        weight_gradient_out(expert)
    combine_other(0)
    combine_other(1)
    for expert in range(EXP_DEV):
        weight_gradient_in(expert)
    combine_own(0, mixed_ref)
    combine_own(1, grad_tokens_ref)

    for copy in (info_copy, grad_copy, token_copy, half_copy(0), half_copy(1)):
        copy.wait_send()
    for t in (0, 1):
        for b in (0, 1):

            def done(j, carry):
                back_copy(t, b, j).wait_send()
                return carry

            lax.fori_loop(1, MATES, done, 0)
        for g in range(count):
            for k in range(STEPS):
                rs_copy(t, g, k).wait_send()
                ag_copy(t, g, k).wait_send()


def layer(tokens, grad_out, info, w_in, w_out):
    tok_rows, width = tokens.shape
    units = w_in.shape[2]
    per_expert = 2 * tok_rows
    total = EXP_DEV * per_expert
    cap = per_expert // (2 * MATES)
    half, full = jnp.bfloat16, jnp.float32
    vmem, dma = pltpu.VMEM, pltpu.SemaphoreType.DMA
    count = len(GROUPS)
    return pl.pallas_call(
        layer_kernel,
        out_shape=(
            jax.ShapeDtypeStruct(tokens.shape, half),
            jax.ShapeDtypeStruct(tokens.shape, half),
            jax.ShapeDtypeStruct(w_in.shape, full),
            jax.ShapeDtypeStruct(w_out.shape, full),
        ),
        in_specs=[pl.BlockSpec(memory_space=vmem)] * 5,
        out_specs=[pl.BlockSpec(memory_space=vmem)] * 4,
        scratch_shapes=[vmem((total, c), half) for c, _ in GROUPS] * 2
        + [vmem((total - total // 16, c), half) for c, _ in GROUPS] * 2
        + [
            vmem((total, units), half),
            vmem((total, units), half),
            vmem((EXP_DEV, per_expert, width), half),
            vmem((EXP_DEV, per_expert, width), half),
            vmem(info.shape, full),
            vmem(tokens.shape, half),
            vmem(tokens.shape, half),
            vmem((2, per_expert, tok_rows), half),
            vmem((2, per_expert, 128), full),
            vmem((2, EXP_DEV, per_expert, width), half),
            vmem((2, 2, MATES, EXP_DEV, cap, width), half),
            vmem((2, tok_rows, width), half),
            vmem((2, tok_rows, width), half),
        ]
        + [dma((2, count, STEPS))] * 4
        + [dma((2, 2, MATES))] * 4
        + [dma((5,))] * 2,
        compiler_params=pltpu.CompilerParams(
            collective_id=0, has_side_effects=True, vmem_limit_bytes=61 * 2**20
        ),
        name="layer",
    )(tokens, grad_out, info, w_in, w_out)


def body(tokens, expert_ids, gate_values, w_in, w_out, grad_out):
    tok_rows = tokens.shape[0]
    num_experts = EXP_DEV * lax.axis_size("expert")
    capacity = 2 * tok_rows * TOP // num_experts
    slots = slot_index(expert_ids, num_experts, capacity).reshape(tok_rows, TOP)
    info = jnp.concatenate(
        [slots.T.astype(jnp.float32), gate_values.T, jnp.zeros((8 - 2 * TOP, tok_rows), jnp.float32)]
    )
    return layer(tokens, grad_out, info, w_in, w_out)


def solution(mesh):
    return jax.shard_map(
        body,
        mesh=mesh,
        in_specs=(
            P("expert", "dp"),
            P("expert", None),
            P("expert", None),
            P("expert", "dp", None),
            P("expert", None, "dp"),
            P("expert", "dp"),
        ),
        out_specs=(
            P("expert", "dp"),
            P("expert", "dp"),
            P("expert", "dp", None),
            P("expert", None, "dp"),
        ),
        check_vma=False,
    )
```

```python
import functools

import jax
import jax.numpy as jnp
from jax import lax
from jax.experimental import pallas as pl
from jax.experimental.pallas import tpu as pltpu
from jax.sharding import PartitionSpec as P

TOP = 2
EXP_DEV = 2
MESH = pl.DeviceIdType.MESH
STEPS = 4
MATES = 8
GROUPS = (
    (0, 256, (1, 0, 2, 3)),
    (0, 256, (0, 1, 2, 3)),
    (0, 256, (2, 0, 1, 3)),
    (0, 256, (2, 1, 0, 3)),
    (0, 256, (0, 1, 2, 3)),
    (0, 256, (1, 0, 2, 3)),
    (1, 256, (0, 1, 2, 3)),
    (1, 256, (1, 0, 2, 3)),
    (1, 256, (2, 1, 0, 3)),
    (1, 256, (2, 0, 1, 3)),
    (1, 256, (0, 1, 2, 3)),
    (1, 256, (1, 0, 2, 3)),
)
FIRST = tuple(sum(q[1] for q in GROUPS[:g] if q[0] == GROUPS[g][0]) for g in range(len(GROUPS)))
ORDER = (
    128, 136, 112, 120, 96, 104, 16, -1, 24, 32, 40, 0, 8, -2, 320, 176, 328, 184, 304, 64, 288, 129, 312, 72,
    296, 48, 208, 160, 216, 168, 224, 17, 232, 25, 192, 33, 200, 41, 321, 56, 368, 1, 376, 177, 209, 185, 217,
    18, 225, 9, 233, 26, 256, 34, 240, 137, 264, 42, 210, 19, 65, 193, 73, 218, 27, 80, 352, 2, 360, 130, 377,
    169, 369, 49, 211, 23, 226, 35, 178, 219, 31, 201, 161, 248, 88, 234, 43, 186, 329, 57, 215, 257, 121,
    227, 39, 194, 3, 10, 223, 322, 131, 138, 235, 47, 265, 66, 370, 241, 74, 50, 361, 113, 378, 231, 179, 38,
    353, 170, 195, 187, 323, 7, 249, 162, 239, 135, 371, 258, 67, 144, 272, 97, 266, 81, 202, 58, 313, 152,
    330, 46, 379, 75, 305, 122, 362, 114, 242, 280, 105, 199, 51, 6, 354, 89, 327, 163, 230, 134, 259, 171,
    267, 71, 250, 243, 59, 273, 82, 37, 238, 314, 45, 289, 98, 30, 306, 22, 355, 167, 363, 175, 263, 79, 251,
    11, 198, 326, 297, 133, 106, 281, 70, 90, 359, 139, 336, 166, 222, 5, 214, 145, 274, 367, 83, 344, 174,
    271, 55, 290, 203, 63, 237, 153, 229, 78, 331, 115, 262, 36, 358, 21, 275, 87, 298, 282, 247, 54, 91, 325,
    165, 197, 132, 255, 62, 123, 366, 69, 337, 44, 146, 270, 4, 307, 183, 279, 86, 99, 283, 95, 315, 191, 246,
    345, 173, 154, 375, 107, 213, 77, 291, 15, 357, 53, 254, 164, 287, 103, 261, 29, 383, 143, 299, 111, 338,
    68, 278, 94, 207, 147, 295, 119, 335, 127, 346, 182, 303, 155, 228, 61, 365, 339, 151, 269, 324, 311, 245,
    85, 52, 319, 126, 221, 118, 253, 347, 159, 236, 60, 196, 343, 286, 150, 93, 318, 125, 351, 374, 158, 310,
    181, 117, 277, 84, 342, 149, 172, 350, 76, 285, 157, 317, 92, 244, 356, 190, 373, 180, 260, 14, 309, 341,
    148, 252, 349, 156, 382, 189, 102, 206, 13, 110, 276, 284, 294, 101, 142, 364, 20, 302, 109, 28, 268, 116,
    205, 334, 124, 381, 188, 12, 348, 372, 141, 301, 293, 100, 108, -3, 340, 380, 333, 140, 292, 204, -4, 300,
    212, 220, 308, 332, -5, 316, -9, -6, -10, -7, -11, -8, -12,
)


def decoded(number):
    rest, k = divmod(number, STEPS)
    rest, gather = divmod(rest, 2)
    rest, g = divmod(rest, len(GROUPS))
    wait, tensor = divmod(rest, 2)
    return wait, tensor, g, gather, k


def gelu_parts(pre):
    scale, cubic = 0.7978845608028654, 0.044715
    square = pre * pre
    tanh = jnp.tanh(scale * (pre + cubic * square * pre))
    half = 0.5 * (1.0 + tanh)
    slope = half + 0.5 * pre * (1.0 - tanh * tanh) * (scale * (1.0 + 3.0 * cubic * square))
    return pre * half, slope


def partners_of(dp):
    x, z = dp // 4, dp % 4
    x0, x1, z0, z1 = x % 2, x // 2, z % 2, z // 2

    def at(a1, a0, c1, c0):
        return (a1 * 2 + a0) * 4 + c1 * 2 + c0

    return (
        (at(x1, 1 - x0, z1, z0), (x0 + x1) % 2),
        (at(1 - x1, 1 - x0, z1, z0), x1),
        (at(x1, x0, z1, 1 - z0), z0),
        (at(x1, x0, 1 - z1, z0), z1),
    )


def layer_kernel(
    tokens_ref, grad_out_ref, ids_ref, gates_ref, w_in_ref, w_out_ref, mixed_ref, grad_tokens_ref, gw_in_out, gw_out_out, *scratch
):
    count = len(GROUPS)
    work = (scratch[0:count], scratch[count : 2 * count])
    recv = (scratch[2 * count : 3 * count], scratch[3 * count : 4 * count])
    (
        act_ref, delta_ref, rows_ref, grads_ref, info_own, info_other, tokens_other, grad_out_other, hot, gate,
        sent, ret, half_sent, half_came, gw_in_ref, gw_out_ref, gw_sem,
        rs_send, rs_recv, ag_send, ag_recv, y_send, y_recv, b_send, b_recv, h_send, h_recv,
    ) = scratch[4 * count :]
    dp, ex = lax.axis_index("dp"), lax.axis_index("expert")
    zh, mate = ex // MATES, ex % MATES
    across = (1 - zh) * MATES + mate
    partners = partners_of(dp)
    tok_rows, width = tokens_ref.shape
    half = rows_ref.shape[2]
    per_expert = 2 * half
    total = EXP_DEV * half
    units = act_ref.shape[2]
    cap = half // MATES
    num_experts = EXP_DEV * 2 * MATES
    outs = (act_ref, delta_ref)
    routed = (rows_ref, grads_ref)

    barrier = pltpu.get_barrier_semaphore()
    for other, _ in partners:
        pl.semaphore_signal(barrier, inc=1, device_id=(other, ex), device_id_type=MESH)
    pl.semaphore_signal(barrier, inc=1, device_id=(dp, across), device_id_type=MESH)
    for j in range(1, MATES):
        near = zh * MATES + (mate + j) % MATES
        pl.semaphore_signal(barrier, inc=1, device_id=(dp, near), device_id_type=MESH)

    def build_map(b):
        source = info_own if b == 0 else info_other
        tile = 128
        expert = lax.broadcasted_iota(jnp.int32, (num_experts, tok_rows), 0).astype(jnp.float32)
        named = [(source[k : k + 1, :] == expert).astype(jnp.float32) for k in range(TOP)]
        earlier = lax.broadcasted_iota(jnp.int32, (tok_rows, tok_rows), 0) < lax.broadcasted_iota(
            jnp.int32, (tok_rows, tok_rows), 1
        )
        before = jnp.dot(
            (named[0] + named[1]).astype(jnp.bfloat16),
            earlier.astype(jnp.float32).astype(jnp.bfloat16),
            preferred_element_type=jnp.float32,
        )
        slots = [
            source[k : k + 1, :] * cap + jnp.sum(named[k] * before, axis=0, keepdims=True) for k in range(TOP)
        ]

        def body(i, carry):
            at = pl.ds(pl.multiple_of(i * tile, tile), tile)
            slot = (
                lax.broadcasted_iota(jnp.int32, (tile, tok_rows), 0) + (zh * per_expert + i * tile)
            ).astype(jnp.float32)
            first, second = slots[0] == slot, slots[1] == slot
            hot[b, at, :] = jnp.where(first, 1.0, jnp.where(second, 1.0, 0.0)).astype(jnp.bfloat16)
            weight = jnp.where(first, source[2:3, :], jnp.where(second, source[3:4, :], 0.0))
            gate[b, at, :] = jnp.broadcast_to(jnp.sum(weight, axis=1, keepdims=True), (tile, 128))
            return carry

        lax.fori_loop(0, per_expert // tile, body, 0)

    def piece(owner):
        return pl.ds(pl.multiple_of(owner * cap, cap), cap)

    def route_copy(tensor, b, j):
        to = (mate + j) % MATES
        return pltpu.make_async_remote_copy(
            src_ref=sent.at[tensor, b, :, piece(to), :],
            dst_ref=routed[tensor].at[b, :, piece(mate), :],
            send_sem=y_send.at[tensor, b, j],
            recv_sem=y_recv.at[tensor, b, j],
            device_id=(dp, zh * MATES + to),
            device_id_type=MESH,
        )

    def route_wait(tensor, b, j):
        return route_copy(tensor, b, j).wait_recv()

    def dispatch(tensor, b):
        block = ((tokens_ref, grad_out_ref), (tokens_other, grad_out_other))[b][tensor]
        near = 4

        def body(i, carry):
            at = pl.ds(pl.multiple_of(i * near * 2 * cap, near * 2 * cap), near * 2 * cap)
            picked = jnp.dot(hot[b, at, :], block[...], preferred_element_type=jnp.float32)
            if tensor == 1:
                level = gate[b, at, :]
                picked = picked * jnp.concatenate([level] * (width // 128), axis=1)
            picked = picked.astype(jnp.bfloat16)
            for n in range(near):
                for e in range(EXP_DEV):
                    start = (n * EXP_DEV + e) * cap
                    sent[tensor, b, e, piece(i * near + n), :] = picked[start : start + cap, :]
            return carry

        lax.fori_loop(0, MATES // near, body, 0)

        def go(j, carry):
            route_copy(tensor, b, j).start()
            return carry

        lax.fori_loop(1, MATES, go, 0)
        routed[tensor][b, :, piece(mate), :] = sent[tensor, b, :, piece(mate), :]

    def arrived(tensor, b):
        def body(j, carry):
            route_wait(tensor, b, j)
            return carry

        lax.fori_loop(1, MATES, body, 0)

    def across_copy(n, source, target):
        return pltpu.make_async_remote_copy(
            src_ref=source,
            dst_ref=target,
            send_sem=h_send.at[n],
            recv_sem=h_recv.at[n],
            device_id=(dp, across),
            device_id_type=MESH,
        )

    def partial_products(tensor, g):
        b, columns, _ = GROUPS[g]
        first = FIRST[g]

        def body(expert, carry):
            if tensor == 0:
                value = jnp.dot(
                    rows_ref[b, expert],
                    w_in_ref[expert, :, first : first + columns],
                    preferred_element_type=jnp.float32,
                )
            else:
                value = lax.dot_general(
                    grads_ref[b, expert],
                    w_out_ref[expert, first : first + columns, :],
                    (((1,), (1,)), ((), ())),
                    preferred_element_type=jnp.float32,
                )
            work[tensor][g][pl.ds(pl.multiple_of(expert * half, half), half), :] = value.astype(jnp.bfloat16)
            return carry

        lax.fori_loop(0, EXP_DEV, body, 0)

    offsets = [[0] for _ in GROUPS]
    for g, (_, _, order) in enumerate(GROUPS):
        for k in range(STEPS):
            offsets[g].append(offsets[g][k] + partners[order[k]][1] * (total >> (k + 1)))

    def rs_copy(tensor, g, k):
        other, bit = partners[GROUPS[g][2][k]]
        size = total >> (k + 1)
        start = pl.multiple_of(offsets[g][k] + (1 - bit) * size, cap)
        return pltpu.make_async_remote_copy(
            src_ref=work[tensor][g].at[pl.ds(start, size), :],
            dst_ref=recv[tensor][g].at[pl.ds(total - 2 * size, size), :],
            send_sem=rs_send.at[tensor, g, k],
            recv_sem=rs_recv.at[tensor, g, k],
            device_id=(other, ex),
            device_id_type=MESH,
        )

    def ag_copy(tensor, g, k):
        other, _ = partners[GROUPS[g][2][k]]
        size = total >> (k + 1)
        held = outs[tensor].at[
            GROUPS[g][0],
            pl.ds(pl.multiple_of(offsets[g][k + 1], cap), size),
            pl.ds(FIRST[g], GROUPS[g][1]),
        ]
        return pltpu.make_async_remote_copy(
            src_ref=held,
            dst_ref=held,
            send_sem=ag_send.at[tensor, g, k],
            recv_sem=ag_recv.at[tensor, g, k],
            device_id=(other, ex),
            device_id_type=MESH,
        )

    def add(tensor, g, k):
        size = total >> (k + 1)
        tile = cap

        def body(i, carry):
            at = pl.ds(pl.multiple_of(offsets[g][k + 1] + i * tile, tile), tile)
            came = pl.ds(pl.multiple_of(total - 2 * size + i * tile, tile), tile)
            mine = work[tensor][g][at, :].astype(jnp.float32)
            work[tensor][g][at, :] = (
                mine + recv[tensor][g][came, :].astype(jnp.float32)
            ).astype(jnp.bfloat16)
            return carry

        lax.fori_loop(0, size // tile, body, 0)

    def activate(g, what):
        b, columns, _ = GROUPS[g]
        size = total >> STEPS
        tile = 32

        def body(i, carry):
            at = pl.ds(pl.multiple_of(offsets[g][STEPS] + i * tile, tile), tile)
            came = pl.ds(pl.multiple_of(total - 2 * size + i * tile, tile), tile)
            for c in range(0, columns, 128):
                part = slice(c, c + 128)
                there = slice(FIRST[g] + c, FIRST[g] + c + 128)
                pre = work[0][g][at, part].astype(jnp.float32) + recv[0][g][came, part].astype(jnp.float32)
                value, slope = gelu_parts(pre)
                if 0 in what:
                    act_ref[b, at, there] = value.astype(jnp.bfloat16)
                if 1 in what:
                    rise = work[1][g][at, part].astype(jnp.float32) + recv[1][g][came, part].astype(jnp.float32)
                    delta_ref[b, at, there] = (rise * slope).astype(jnp.bfloat16)
            return carry

        lax.fori_loop(0, size // tile, body, 0)

    def back_copy(tensor, b, j):
        to = (mate + j) % MATES
        return pltpu.make_async_remote_copy(
            src_ref=sent.at[tensor, b, :, piece(to), :],
            dst_ref=ret.at[tensor, b, mate],
            send_sem=b_send.at[tensor, b, j],
            recv_sem=b_recv.at[tensor, b, j],
            device_id=(dp, zh * MATES + to),
            device_id_type=MESH,
        )

    def results(tensor, b):
        def left(j, carry):
            route_copy(tensor, b, j).wait_send()
            return carry

        lax.fori_loop(1, MATES, left, 0)

        def body(expert, carry):
            at = pl.ds(pl.multiple_of(expert * half, half), half)
            if tensor == 0:
                value = jnp.dot(act_ref[b, at, :], w_out_ref[expert], preferred_element_type=jnp.float32)
            else:
                value = lax.dot_general(
                    delta_ref[b, at, :],
                    w_in_ref[expert],
                    (((1,), (1,)), ((), ())),
                    preferred_element_type=jnp.float32,
                )
            sent[tensor, b, expert] = value.astype(jnp.bfloat16)
            return carry

        lax.fori_loop(0, EXP_DEV, body, 0)

        def go(j, carry):
            back_copy(tensor, b, j).start()
            return carry

        lax.fori_loop(1, MATES, go, 0)
        ret[tensor, b, mate] = sent[tensor, b, :, piece(mate), :]

    def combine(tensor, b):
        def body(j, carry):
            back_copy(tensor, b, j).wait_recv()
            return carry

        lax.fori_loop(1, MATES, body, 0)
        value = ret[tensor, b].reshape(per_expert, width)
        over_slots = (((0,), (0,)), ((), ()))
        if tensor == 1:
            return lax.dot_general(hot[b], value, over_slots, preferred_element_type=jnp.float32)
        level = gate[b]
        value = value.astype(jnp.float32) * jnp.concatenate([level] * (width // 128), axis=1)
        high = value.astype(jnp.bfloat16)
        low = (value - high.astype(jnp.float32)).astype(jnp.bfloat16)
        return lax.dot_general(
            hot[b], high, over_slots, preferred_element_type=jnp.float32
        ) + lax.dot_general(hot[b], low, over_slots, preferred_element_type=jnp.float32)

    def half_copy(tensor):
        return across_copy(3 + tensor, half_sent.at[tensor], half_came.at[tensor])

    def combine_other(tensor):
        half_sent[tensor] = combine(tensor, 1).astype(jnp.bfloat16)
        half_copy(tensor).start()

    def combine_own(tensor, out_ref):
        mine = combine(tensor, 0)
        half_copy(tensor).wait_recv()
        out_ref[...] = (mine + half_came[tensor].astype(jnp.float32)).astype(jnp.bfloat16)

    def weight_gradient(tensor, expert, part):
        tile = 256
        parts = units // tile // 2
        over_rows = (((0,), (0,)), ((), ()))

        def product(left, right):
            return lax.dot_general(left, right, over_rows, preferred_element_type=jnp.float32)

        def body(i, carry):
            columns = pl.ds(pl.multiple_of((part * parts + i) * tile, tile), tile)
            rows = pl.ds(expert * half, half)
            if tensor == 0:
                gw_out_ref[expert, columns, :] = product(act_ref[0, rows, columns], grads_ref[0, expert]) + product(
                    act_ref[1, rows, columns], grads_ref[1, expert]
                )
            else:
                gw_in_ref[expert, :, columns] = product(rows_ref[0, expert], delta_ref[0, rows, columns]) + product(
                    rows_ref[1, expert], delta_ref[1, rows, columns]
                )
            return carry

        lax.fori_loop(0, parts, body, 0)
        weight_copy(tensor, expert, part).start()

    def weight_copy(tensor, expert, part):
        columns = pl.ds(part * (units // 2), units // 2)
        source, target = ((gw_out_ref, gw_out_out), (gw_in_ref, gw_in_out))[tensor]
        place = (expert, columns, slice(None)) if tensor == 0 else (expert, slice(None), columns)
        return pltpu.make_async_copy(source.at[place], target.at[place], gw_sem.at[tensor, expert, part])

    pl.semaphore_wait(barrier, len(partners) + MATES)
    info_copy = across_copy(0, info_own, info_other)
    grad_copy = across_copy(1, grad_out_ref, grad_out_other)
    token_copy = across_copy(2, tokens_ref, tokens_other)
    info_own[0:TOP, :] = ids_ref[...].astype(jnp.float32)
    info_own[TOP : 2 * TOP, :] = gates_ref[...]
    info_own[2 * TOP :, :] = jnp.zeros((8 - 2 * TOP, tok_rows), jnp.float32)
    info_copy.start()
    grad_copy.start()
    token_copy.start()
    build_map(0)
    dispatch(1, 0)
    dispatch(0, 0)

    seen = set()

    def other_grads():
        info_copy.wait_recv()
        build_map(1)
        grad_copy.wait_recv()
        dispatch(1, 1)

    def other_tokens():
        token_copy.wait_recv()
        dispatch(0, 1)

    extra = {
        -1: other_grads,
        -2: other_tokens,
        -3: functools.partial(combine_other, 0),
        -4: functools.partial(combine_other, 1),
    }
    for n in range(4):
        extra[-5 - n] = functools.partial(weight_gradient, 0, n // 2, n % 2)
        extra[-9 - n] = functools.partial(weight_gradient, 1, n // 2, n % 2)
    for number in ORDER:
        if number < 0:
            extra[number]()
            continue
        wait, tensor, g, gather, k = decoded(number)
        b = GROUPS[g][0]
        if not wait and not gather and k == 0:
            if (tensor, b) not in seen:
                seen.add((tensor, b))
                arrived(tensor, b)
            partial_products(tensor, g)
        copy = (ag_copy if gather else rs_copy)(tensor, g, k)
        if not wait:
            copy.start()
            continue
        copy.wait_recv()
        seen.add((tensor, g, gather, k))
        if gather:
            if k == 0 and all((tensor, n, 1, 0) in seen for n in range(count) if GROUPS[n][0] == b):
                results(tensor, b)
        elif k < STEPS - 1:
            add(tensor, g, k)
        elif tensor == 0:
            activate(g, (0, 1) if (1, g, 0, k) in seen else (0,))
        elif (0, g, 0, k) in seen:
            activate(g, (1,))
    combine_own(0, mixed_ref)
    combine_own(1, grad_tokens_ref)

    for copy in (info_copy, grad_copy, token_copy, half_copy(0), half_copy(1)):
        copy.wait_send()
    for t in (0, 1):
        for expert in range(EXP_DEV):
            for part in (0, 1):
                weight_copy(t, expert, part).wait()
        for b in (0, 1):

            def done(j, carry):
                back_copy(t, b, j).wait_send()
                return carry

            lax.fori_loop(1, MATES, done, 0)
        for g in range(count):
            for k in range(STEPS):
                rs_copy(t, g, k).wait_send()
                ag_copy(t, g, k).wait_send()


def layer(tokens, grad_out, ids, gates, w_in, w_out):
    tok_rows, width = tokens.shape
    units = w_in.shape[2]
    per_expert = 2 * tok_rows
    total = EXP_DEV * tok_rows
    cap = tok_rows // MATES
    info = (8, tok_rows)
    half, full = jnp.bfloat16, jnp.float32
    vmem, dma = pltpu.VMEM, pltpu.SemaphoreType.DMA
    count = len(GROUPS)
    return pl.pallas_call(
        layer_kernel,
        out_shape=(
            jax.ShapeDtypeStruct(tokens.shape, half),
            jax.ShapeDtypeStruct(tokens.shape, half),
            jax.ShapeDtypeStruct(w_in.shape, full),
            jax.ShapeDtypeStruct(w_out.shape, full),
        ),
        in_specs=[pl.BlockSpec(memory_space=vmem)] * 6,
        out_specs=[pl.BlockSpec(memory_space=vmem)] * 2 + [pl.BlockSpec(memory_space=pl.ANY)] * 2,
        scratch_shapes=[vmem((total, c), half) for _, c, _ in GROUPS] * 2
        + [vmem((total - total // 16, c), half) for _, c, _ in GROUPS] * 2
        + [
            vmem((2, total, units), half),
            vmem((2, total, units), half),
            vmem((2, EXP_DEV, tok_rows, width), half),
            vmem((2, EXP_DEV, tok_rows, width), half),
            vmem(info, full),
            vmem(info, full),
            vmem(tokens.shape, half),
            vmem(tokens.shape, half),
            vmem((2, per_expert, tok_rows), half),
            vmem((2, per_expert, 128), full),
            vmem((2, 2, EXP_DEV, tok_rows, width), half),
            vmem((2, 2, MATES, EXP_DEV, cap, width), half),
            vmem((2, tok_rows, width), half),
            vmem((2, tok_rows, width), half),
            vmem(w_in.shape, full),
            vmem(w_out.shape, full),
            dma((2, EXP_DEV, 2)),
        ]
        + [dma((2, count, STEPS))] * 4
        + [dma((2, 2, MATES))] * 4
        + [dma((5,))] * 2,
        compiler_params=pltpu.CompilerParams(
            collective_id=0, has_side_effects=True, vmem_limit_bytes=61 * 2**20
        ),
        name="layer",
    )(tokens, grad_out, ids, gates, w_in, w_out)


def body(tokens, expert_ids, gate_values, w_in, w_out, grad_out):
    return layer(tokens, grad_out, expert_ids.T, gate_values.T, w_in, w_out)


def solution(mesh):
    return jax.shard_map(
        body,
        mesh=mesh,
        in_specs=(
            P("expert", "dp"),
            P("expert", None),
            P("expert", None),
            P("expert", "dp", None),
            P("expert", None, "dp"),
            P("expert", "dp"),
        ),
        out_specs=(
            P("expert", "dp"),
            P("expert", "dp"),
            P("expert", "dp", None),
            P("expert", None, "dp"),
        ),
        check_vma=False,
    )
```

```python
import functools

import jax
import jax.numpy as jnp
from jax import lax
from jax.experimental import pallas as pl
from jax.experimental.pallas import tpu as pltpu
from jax.sharding import PartitionSpec as P

TOP = 2
EXP_DEV = 2
MESH = pl.DeviceIdType.MESH
STEPS = 4
MATES = 8
GROUPS = (
    (0, 256, (0, 1, 2, 3)),
    (0, 256, (1, 0, 2, 3)),
    (0, 256, (0, 1, 2, 3)),
    (0, 256, (1, 0, 2, 3)),
    (0, 256, (1, 0, 3, 2)),
    (0, 256, (0, 1, 3, 2)),
    (1, 256, (2, 0, 1, 3)),
    (1, 256, (2, 1, 0, 3)),
    (1, 256, (0, 1, 2, 3)),
    (1, 256, (1, 0, 2, 3)),
    (1, 256, (1, 0, 2, 3)),
    (1, 256, (0, 1, 2, 3)),
)
FIRST = tuple(sum(q[1] for q in GROUPS[:g] if q[0] == GROUPS[g][0]) for g in range(len(GROUPS)))
ORDER = (
    96, 104, 112, 120, 128, 136, -1, 288, 40, 296, 97, 304, 105, 328, 0, 312, 113, 320, 32, 144, 152, 289, 98,
    137, 297, 121, 305, 8, -2, 232, 129, 290, 99, 106, 329, 41, 138, 192, 184, 291, 224, 1, 313, 33, 330, 321,
    130, 64, 298, 107, 114, 233, 42, 72, 336, 122, 344, 139, 200, 80, 193, 176, 306, 2, 299, 115, 322, 225,
    34, 9, 331, 131, 234, 376, 88, 314, 123, 43, 307, 194, 3, 48, 323, 56, 226, 235, 35, 256, 16, 315, 195, 7,
    103, 201, 145, 264, 65, 227, 10, 272, 185, 368, 24, 199, 295, 280, 73, 257, 89, 202, 6, 11, 337, 81, 240,
    66, 377, 146, 203, 15, 111, 248, 186, 208, 177, 198, 39, 265, 49, 258, 67, 74, 273, 160, 281, 5, 338, 17,
    216, 57, 207, 147, 303, 259, 71, 231, 14, 38, 378, 82, 266, 90, 339, 75, 369, 25, 197, 153, 241, 4, 263,
    187, 209, 50, 249, 168, 230, 267, 79, 206, 70, 379, 274, 83, 178, 345, 282, 91, 18, 352, 13, 161, 242,
    217, 37, 271, 51, 275, 87, 283, 95, 262, 69, 78, 243, 55, 196, 58, 370, 26, 360, 210, 47, 279, 179, 353,
    287, 19, 205, 12, 154, 247, 54, 191, 229, 169, 270, 86, 261, 36, 250, 68, 371, 59, 239, 94, 346, 77, 211,
    46, 218, 162, 383, 27, 278, 190, 246, 251, 63, 361, 85, 286, 93, 170, 219, 155, 238, 183, 255, 151, 269,
    53, 204, 76, 354, 135, 382, 143, 228, 45, 362, 102, 347, 163, 260, 62, 375, 171, 277, 343, 159, 285, 84,
    92, 327, 182, 335, 110, 245, 294, 52, 254, 355, 167, 363, 175, 351, 158, 134, 237, 61, 44, 374, 302, 284,
    181, 359, 166, 142, 350, 109, 268, 189, 367, 174, 23, 326, 31, 253, 150, 276, 157, 215, 119, 334, 127,
    373, 133, 381, 180, 223, 358, 60, 366, 22, 301, 173, 342, 165, 311, 319, 236, 188, 244, 30, 349, 141, 325,
    149, 214, 156, 222, 118, 365, 29, 357, 172, 372, 132, 252, 126, 333, 21, 310, 341, 164, 148, 380, 140,
    221, 348, 318, 125, 340, 213, 28, 364, 117, -3, 324, 101, 356, 20, 317, 332, 309, 116, 124, 212, 293, 100,
    108, 220, -5, -4, -6, -7, 308, -8, 292, 316, 300, -9, -10, -11, -12,
)


def decoded(number):
    rest, k = divmod(number, STEPS)
    rest, gather = divmod(rest, 2)
    rest, g = divmod(rest, len(GROUPS))
    wait, tensor = divmod(rest, 2)
    return wait, tensor, g, gather, k


def gelu_parts(pre):
    scale, cubic = 0.7978845608028654, 0.044715
    square = pre * pre
    tanh = jnp.tanh(scale * (pre + cubic * square * pre))
    half = 0.5 * (1.0 + tanh)
    slope = half + 0.5 * pre * (1.0 - tanh * tanh) * (scale * (1.0 + 3.0 * cubic * square))
    return pre * half, slope


def partners_of(dp):
    x, z = dp // 4, dp % 4
    x0, x1, z0, z1 = x % 2, x // 2, z % 2, z // 2

    def at(a1, a0, c1, c0):
        return (a1 * 2 + a0) * 4 + c1 * 2 + c0

    return (
        (at(x1, 1 - x0, z1, z0), (x0 + x1) % 2),
        (at(1 - x1, 1 - x0, z1, z0), x1),
        (at(x1, x0, z1, 1 - z0), z0),
        (at(x1, x0, 1 - z1, z0), z1),
    )


def layer_kernel(
    tokens_ref, grad_out_ref, ids_ref, gates_ref, w_in_arg, w_out_arg, mixed_ref, grad_tokens_ref, gw_in_out, gw_out_out, *scratch
):
    count = len(GROUPS)
    work = (scratch[0:count], scratch[count : 2 * count])
    recv = (scratch[2 * count : 3 * count], scratch[3 * count : 4 * count])
    (
        rows_ref, grads_ref, info_own, info_other, tokens_other, grad_out_other, hot, gate,
        sent, ret, half_sent, half_came, gw_in_ref, gw_out_ref, gw_sem, w_in_ref, w_out_ref, w_sem,
        rs_send, rs_recv, ag_send, ag_recv, y_send, y_recv, b_send, b_recv, h_send, h_recv,
    ) = scratch[6 * count :]
    dp, ex = lax.axis_index("dp"), lax.axis_index("expert")
    zh, mate = ex // MATES, ex % MATES
    across = (1 - zh) * MATES + mate
    partners = partners_of(dp)
    tok_rows, width = tokens_ref.shape
    half = rows_ref.shape[2]
    per_expert = 2 * half
    total = EXP_DEV * half
    units = w_in_ref.shape[2]
    cap = half // MATES
    num_experts = EXP_DEV * 2 * MATES
    outs = (scratch[4 * count : 5 * count], scratch[5 * count : 6 * count])
    routed = (rows_ref, grads_ref)

    weights_in = pltpu.make_async_copy(w_in_arg, w_in_ref, w_sem.at[0])
    weights_out = pltpu.make_async_copy(w_out_arg, w_out_ref, w_sem.at[1])
    weights_out.start()
    weights_in.start()

    barrier = pltpu.get_barrier_semaphore()
    for other, _ in partners:
        pl.semaphore_signal(barrier, inc=1, device_id=(other, ex), device_id_type=MESH)
    pl.semaphore_signal(barrier, inc=1, device_id=(dp, across), device_id_type=MESH)
    for j in range(1, MATES):
        near = zh * MATES + (mate + j) % MATES
        pl.semaphore_signal(barrier, inc=1, device_id=(dp, near), device_id_type=MESH)

    def build_map(b):
        source = info_own if b == 0 else info_other
        tile = 128
        expert = lax.broadcasted_iota(jnp.int32, (num_experts, tok_rows), 0).astype(jnp.float32)
        named = [(source[k : k + 1, :] == expert).astype(jnp.float32) for k in range(TOP)]
        earlier = lax.broadcasted_iota(jnp.int32, (tok_rows, tok_rows), 0) < lax.broadcasted_iota(
            jnp.int32, (tok_rows, tok_rows), 1
        )
        before = jnp.dot(
            (named[0] + named[1]).astype(jnp.bfloat16),
            earlier.astype(jnp.float32).astype(jnp.bfloat16),
            preferred_element_type=jnp.float32,
        )
        slots = [
            source[k : k + 1, :] * cap + jnp.sum(named[k] * before, axis=0, keepdims=True) for k in range(TOP)
        ]

        def body(i, carry):
            at = pl.ds(pl.multiple_of(i * tile, tile), tile)
            slot = (
                lax.broadcasted_iota(jnp.int32, (tile, tok_rows), 0) + (zh * per_expert + i * tile)
            ).astype(jnp.float32)
            first, second = slots[0] == slot, slots[1] == slot
            hot[b, at, :] = jnp.where(first, 1.0, jnp.where(second, 1.0, 0.0)).astype(jnp.bfloat16)
            weight = jnp.where(first, source[2:3, :], jnp.where(second, source[3:4, :], 0.0))
            gate[b, at, :] = jnp.broadcast_to(jnp.sum(weight, axis=1, keepdims=True), (tile, 128))
            return carry

        lax.fori_loop(0, per_expert // tile, body, 0)

    def piece(owner):
        return pl.ds(pl.multiple_of(owner * cap, cap), cap)

    def route_copy(tensor, b, j):
        to = (mate + j) % MATES
        return pltpu.make_async_remote_copy(
            src_ref=sent.at[tensor, b, :, piece(to), :],
            dst_ref=routed[tensor].at[b, :, piece(mate), :],
            send_sem=y_send.at[tensor, b, j],
            recv_sem=y_recv.at[tensor, b, j],
            device_id=(dp, zh * MATES + to),
            device_id_type=MESH,
        )

    def route_wait(tensor, b, j):
        return route_copy(tensor, b, j).wait_recv()

    def dispatch(tensor, b):
        block = ((tokens_ref, grad_out_ref), (tokens_other, grad_out_other))[b][tensor]
        near = 4

        def body(i, carry):
            at = pl.ds(pl.multiple_of(i * near * 2 * cap, near * 2 * cap), near * 2 * cap)
            picked = jnp.dot(hot[b, at, :], block[...], preferred_element_type=jnp.float32)
            if tensor == 1:
                level = gate[b, at, :]
                picked = picked * jnp.concatenate([level] * (width // 128), axis=1)
            picked = picked.astype(jnp.bfloat16)
            for n in range(near):
                for e in range(EXP_DEV):
                    start = (n * EXP_DEV + e) * cap
                    sent[tensor, b, e, piece(i * near + n), :] = picked[start : start + cap, :]
            return carry

        lax.fori_loop(0, MATES // near, body, 0)

        def go(j, carry):
            route_copy(tensor, b, j).start()
            return carry

        lax.fori_loop(1, MATES, go, 0)
        routed[tensor][b, :, piece(mate), :] = sent[tensor, b, :, piece(mate), :]

    def arrived(tensor, b):
        def body(j, carry):
            route_wait(tensor, b, j)
            return carry

        lax.fori_loop(1, MATES, body, 0)

    def across_copy(n, source, target):
        return pltpu.make_async_remote_copy(
            src_ref=source,
            dst_ref=target,
            send_sem=h_send.at[n],
            recv_sem=h_recv.at[n],
            device_id=(dp, across),
            device_id_type=MESH,
        )

    def partial_products(tensor, g):
        b, columns, _ = GROUPS[g]
        first = FIRST[g]

        def body(expert, carry):
            if tensor == 0:
                value = jnp.dot(
                    rows_ref[b, expert],
                    w_in_ref[expert, :, first : first + columns],
                    preferred_element_type=jnp.float32,
                )
            else:
                value = lax.dot_general(
                    grads_ref[b, expert],
                    w_out_ref[expert, first : first + columns, :],
                    (((1,), (1,)), ((), ())),
                    preferred_element_type=jnp.float32,
                )
            work[tensor][g][pl.ds(pl.multiple_of(expert * half, half), half), :] = value.astype(jnp.bfloat16)
            return carry

        lax.fori_loop(0, EXP_DEV, body, 0)

    offsets = [[0] for _ in GROUPS]
    for g, (_, _, order) in enumerate(GROUPS):
        for k in range(STEPS):
            offsets[g].append(offsets[g][k] + partners[order[k]][1] * (total >> (k + 1)))

    def rs_copy(tensor, g, k):
        other, bit = partners[GROUPS[g][2][k]]
        size = total >> (k + 1)
        start = pl.multiple_of(offsets[g][k] + (1 - bit) * size, cap)
        return pltpu.make_async_remote_copy(
            src_ref=work[tensor][g].at[pl.ds(start, size), :],
            dst_ref=recv[tensor][g].at[pl.ds(total - 2 * size, size), :],
            send_sem=rs_send.at[tensor, g, k],
            recv_sem=rs_recv.at[tensor, g, k],
            device_id=(other, ex),
            device_id_type=MESH,
        )

    def ag_copy(tensor, g, k):
        other, _ = partners[GROUPS[g][2][k]]
        size = total >> (k + 1)
        held = outs[tensor][g].at[pl.ds(pl.multiple_of(offsets[g][k + 1], cap), size), :]
        return pltpu.make_async_remote_copy(
            src_ref=held,
            dst_ref=held,
            send_sem=ag_send.at[tensor, g, k],
            recv_sem=ag_recv.at[tensor, g, k],
            device_id=(other, ex),
            device_id_type=MESH,
        )

    def add(tensor, g, k):
        size = total >> (k + 1)
        tile = cap

        def body(i, carry):
            at = pl.ds(pl.multiple_of(offsets[g][k + 1] + i * tile, tile), tile)
            came = pl.ds(pl.multiple_of(total - 2 * size + i * tile, tile), tile)
            mine = work[tensor][g][at, :].astype(jnp.float32)
            work[tensor][g][at, :] = (
                mine + recv[tensor][g][came, :].astype(jnp.float32)
            ).astype(jnp.bfloat16)
            return carry

        lax.fori_loop(0, size // tile, body, 0)

    def activate(g, what):
        columns = GROUPS[g][1]
        size = total >> STEPS
        tile = 32

        def body(i, carry):
            at = pl.ds(pl.multiple_of(offsets[g][STEPS] + i * tile, tile), tile)
            came = pl.ds(pl.multiple_of(total - 2 * size + i * tile, tile), tile)
            for c in range(0, columns, 128):
                part = slice(c, c + 128)
                pre = work[0][g][at, part].astype(jnp.float32) + recv[0][g][came, part].astype(jnp.float32)
                value, slope = gelu_parts(pre)
                if 0 in what:
                    outs[0][g][at, part] = value.astype(jnp.bfloat16)
                if 1 in what:
                    rise = work[1][g][at, part].astype(jnp.float32) + recv[1][g][came, part].astype(jnp.float32)
                    outs[1][g][at, part] = (rise * slope).astype(jnp.bfloat16)
            return carry

        lax.fori_loop(0, size // tile, body, 0)

    def back_copy(tensor, b, j):
        to = (mate + j) % MATES
        return pltpu.make_async_remote_copy(
            src_ref=sent.at[tensor, b, :, piece(to), :],
            dst_ref=ret.at[tensor, b, mate],
            send_sem=b_send.at[tensor, b, j],
            recv_sem=b_recv.at[tensor, b, j],
            device_id=(dp, zh * MATES + to),
            device_id_type=MESH,
        )

    def results(tensor, b):
        def left(j, carry):
            route_copy(tensor, b, j).wait_send()
            return carry

        lax.fori_loop(1, MATES, left, 0)

        def body(expert, carry):
            at = pl.ds(pl.multiple_of(expert * half, half), half)
            value = 0.0
            for g in range(count):
                if GROUPS[g][0] != b:
                    continue
                part = slice(FIRST[g], FIRST[g] + GROUPS[g][1])
                if tensor == 0:
                    value += jnp.dot(
                        outs[0][g][at, :], w_out_ref[expert, part, :], preferred_element_type=jnp.float32
                    )
                else:
                    value += lax.dot_general(
                        outs[1][g][at, :],
                        w_in_ref[expert, :, part],
                        (((1,), (1,)), ((), ())),
                        preferred_element_type=jnp.float32,
                    )
            sent[tensor, b, expert] = value.astype(jnp.bfloat16)
            return carry

        lax.fori_loop(0, EXP_DEV, body, 0)

        def go(j, carry):
            back_copy(tensor, b, j).start()
            return carry

        lax.fori_loop(1, MATES, go, 0)
        ret[tensor, b, mate] = sent[tensor, b, :, piece(mate), :]

    def combine(tensor, b):
        def body(j, carry):
            back_copy(tensor, b, j).wait_recv()
            return carry

        lax.fori_loop(1, MATES, body, 0)
        value = ret[tensor, b].reshape(per_expert, width)
        over_slots = (((0,), (0,)), ((), ()))
        if tensor == 1:
            return lax.dot_general(hot[b], value, over_slots, preferred_element_type=jnp.float32)
        level = gate[b]
        value = value.astype(jnp.float32) * jnp.concatenate([level] * (width // 128), axis=1)
        high = value.astype(jnp.bfloat16)
        low = (value - high.astype(jnp.float32)).astype(jnp.bfloat16)
        return lax.dot_general(
            hot[b], high, over_slots, preferred_element_type=jnp.float32
        ) + lax.dot_general(hot[b], low, over_slots, preferred_element_type=jnp.float32)

    def half_copy(tensor):
        return across_copy(3 + tensor, half_sent.at[tensor], half_came.at[tensor])

    def combine_other(tensor):
        half_sent[tensor] = combine(tensor, 1).astype(jnp.bfloat16)
        half_copy(tensor).start()

    def combine_own(tensor, out_ref):
        mine = combine(tensor, 0)
        half_copy(tensor).wait_recv()
        out_ref[...] = (mine + half_came[tensor].astype(jnp.float32)).astype(jnp.bfloat16)

    def weight_gradient(tensor, expert, part):
        over_rows = (((0,), (0,)), ((), ()))
        pairs = [(n, n + count // 2) for n in range(count // 2)]
        rows = slice(expert * half, (expert + 1) * half)

        def product(left, right):
            return lax.dot_general(left, right, over_rows, preferred_element_type=jnp.float32)

        for pair in pairs[part * count // 4 : (part + 1) * count // 4]:
            columns = slice(FIRST[pair[0]], FIRST[pair[0]] + GROUPS[pair[0]][1])
            if tensor == 0:
                gw_out_ref[expert, columns, :] = sum(
                    product(outs[0][g][rows, :], grads_ref[GROUPS[g][0], expert]) for g in pair
                )
            else:
                gw_in_ref[expert, :, columns] = sum(
                    product(rows_ref[GROUPS[g][0], expert], outs[1][g][rows, :]) for g in pair
                )
        weight_copy(tensor, expert, part).start()

    def weight_copy(tensor, expert, part):
        columns = pl.ds(part * (units // 2), units // 2)
        source, target = ((gw_out_ref, gw_out_out), (gw_in_ref, gw_in_out))[tensor]
        place = (expert, columns, slice(None)) if tensor == 0 else (expert, slice(None), columns)
        return pltpu.make_async_copy(source.at[place], target.at[place], gw_sem.at[tensor, expert, part])

    pl.semaphore_wait(barrier, len(partners) + MATES)
    info_copy = across_copy(0, info_own, info_other)
    grad_copy = across_copy(1, grad_out_ref, grad_out_other)
    token_copy = across_copy(2, tokens_ref, tokens_other)
    info_own[0:TOP, :] = ids_ref[...].astype(jnp.float32)
    info_own[TOP : 2 * TOP, :] = gates_ref[...]
    info_own[2 * TOP :, :] = jnp.zeros((8 - 2 * TOP, tok_rows), jnp.float32)
    info_copy.start()
    grad_copy.start()
    build_map(0)
    dispatch(1, 0)
    dispatch(0, 0)
    weights_out.wait()
    weights_in.wait()

    seen = set()

    def other_grads():
        grad_copy.wait_recv()
        token_copy.start()
        info_copy.wait_recv()
        build_map(1)
        dispatch(1, 1)

    def other_tokens():
        token_copy.wait_recv()
        dispatch(0, 1)

    extra = {
        -1: other_grads,
        -2: other_tokens,
        -3: functools.partial(combine_other, 0),
        -4: functools.partial(combine_other, 1),
    }
    for n in range(4):
        extra[-5 - n] = functools.partial(weight_gradient, 0, n // 2, n % 2)
        extra[-9 - n] = functools.partial(weight_gradient, 1, n // 2, n % 2)
    for number in ORDER:
        if number < 0:
            extra[number]()
            continue
        wait, tensor, g, gather, k = decoded(number)
        b = GROUPS[g][0]
        if not wait and not gather and k == 0:
            if (tensor, b) not in seen:
                seen.add((tensor, b))
                arrived(tensor, b)
            partial_products(tensor, g)
        copy = (ag_copy if gather else rs_copy)(tensor, g, k)
        if not wait:
            copy.start()
            continue
        copy.wait_recv()
        seen.add((tensor, g, gather, k))
        if gather:
            if k == 0 and all((tensor, n, 1, 0) in seen for n in range(count) if GROUPS[n][0] == b):
                results(tensor, b)
        elif k < STEPS - 1:
            add(tensor, g, k)
        elif tensor == 0:
            activate(g, (0, 1) if (1, g, 0, k) in seen else (0,))
        elif (0, g, 0, k) in seen:
            activate(g, (1,))
    combine_own(0, mixed_ref)
    combine_own(1, grad_tokens_ref)

    for copy in (info_copy, grad_copy, token_copy, half_copy(0), half_copy(1)):
        copy.wait_send()
    for t in (0, 1):
        for expert in range(EXP_DEV):
            for part in (0, 1):
                weight_copy(t, expert, part).wait()
        for b in (0, 1):

            def done(j, carry):
                back_copy(t, b, j).wait_send()
                return carry

            lax.fori_loop(1, MATES, done, 0)
        for g in range(count):
            for k in range(STEPS):
                rs_copy(t, g, k).wait_send()
                ag_copy(t, g, k).wait_send()


def layer(tokens, grad_out, ids, gates, w_in, w_out):
    tok_rows, width = tokens.shape
    per_expert = 2 * tok_rows
    total = EXP_DEV * tok_rows
    cap = tok_rows // MATES
    info = (8, tok_rows)
    half, full = jnp.bfloat16, jnp.float32
    vmem, dma = pltpu.VMEM, pltpu.SemaphoreType.DMA
    count = len(GROUPS)
    return pl.pallas_call(
        layer_kernel,
        out_shape=(
            jax.ShapeDtypeStruct(tokens.shape, half),
            jax.ShapeDtypeStruct(tokens.shape, half),
            jax.ShapeDtypeStruct(w_in.shape, full),
            jax.ShapeDtypeStruct(w_out.shape, full),
        ),
        in_specs=[pl.BlockSpec(memory_space=vmem)] * 4 + [pl.BlockSpec(memory_space=pl.ANY)] * 2,
        out_specs=[pl.BlockSpec(memory_space=vmem)] * 2 + [pl.BlockSpec(memory_space=pl.ANY)] * 2,
        scratch_shapes=[vmem((total, c), half) for _, c, _ in GROUPS] * 2
        + [vmem((total - total // 16, c), half) for _, c, _ in GROUPS] * 2
        + [vmem((total, c), half) for _, c, _ in GROUPS] * 2
        + [
            vmem((2, EXP_DEV, tok_rows, width), half),
            vmem((2, EXP_DEV, tok_rows, width), half),
            vmem(info, full),
            vmem(info, full),
            vmem(tokens.shape, half),
            vmem(tokens.shape, half),
            vmem((2, per_expert, tok_rows), half),
            vmem((2, per_expert, 128), full),
            vmem((2, 2, EXP_DEV, tok_rows, width), half),
            vmem((2, 2, MATES, EXP_DEV, cap, width), half),
            vmem((2, tok_rows, width), half),
            vmem((2, tok_rows, width), half),
            vmem(w_in.shape, full),
            vmem(w_out.shape, full),
            dma((2, EXP_DEV, 2)),
            vmem(w_in.shape, half),
            vmem(w_out.shape, half),
            dma((2,)),
        ]
        + [dma((2, count, STEPS))] * 4
        + [dma((2, 2, MATES))] * 4
        + [dma((5,))] * 2,
        compiler_params=pltpu.CompilerParams(
            collective_id=0, has_side_effects=True, vmem_limit_bytes=61 * 2**20
        ),
        name="layer",
    )(tokens, grad_out, ids, gates, w_in, w_out)


def publish_kernel(*refs):
    count = len(refs) // 2
    for source, target in zip(refs[:count], refs[count:]):
        target[...] = source[...]


def publish(*arrays):
    steps = 8

    def block(a):
        shape = (*a.shape[:-2], a.shape[-2] // steps, a.shape[-1])
        if len(shape) == 3:
            return pl.BlockSpec(shape, lambda i: (0, i, 0))
        return pl.BlockSpec(shape, lambda i: (i, 0))

    return pl.pallas_call(
        publish_kernel,
        grid=(steps,),
        out_shape=tuple(jax.ShapeDtypeStruct(a.shape, a.dtype) for a in arrays),
        in_specs=[block(a) for a in arrays],
        out_specs=[block(a) for a in arrays],
        name="publish",
    )(*arrays)


def body(tokens, expert_ids, gate_values, w_in, w_out, grad_out):
    return publish(*layer(tokens, grad_out, expert_ids.T, gate_values.T, w_in, w_out))


def solution(mesh):
    return jax.shard_map(
        body,
        mesh=mesh,
        in_specs=(
            P("expert", "dp"),
            P("expert", None),
            P("expert", None),
            P("expert", "dp", None),
            P("expert", None, "dp"),
            P("expert", "dp"),
        ),
        out_specs=(
            P("expert", "dp"),
            P("expert", "dp"),
            P("expert", "dp", None),
            P("expert", None, "dp"),
        ),
        check_vma=False,
    )
```
